256 devices in a mesh: rep: 32 (over x, z), fsdp: 8 (over y, core).
Axes of the slice: x: 4, y: 4, z: 8, core: 2. Of those that a mesh axis runs over, the one named last changes fastest.
Arguments:
- grad_parts: bfloat16 [32, 8, 2097152], P('rep', 'fsdp'), may hold values from -6 to 6
- momentum: float32 [32, 2097152], P('rep', 'fsdp'), may hold values from -6 to 6
- bands: int32 [32, 4096, 32], P('rep', 'fsdp'), may hold values from 0 to 63, as said below
- counts: int32 [32, 4096], P('rep', 'fsdp'), may hold values from 1 to 32
Outputs:
- new_momentum: float32 [32, 2097152], P('rep', 'fsdp')
- update: float32 [2097152], P('fsdp')
The draws below stay inside these ranges and needn't reach their ends.
Inputs may be any that keep to these rules, and one draw needn't show every extreme that they name: `bands`: in each list the 32 entries are distinct frequencies; entries at positions counts and beyond are ignored.
All inputs are finite; a program needn't handle non-finite values.
Results may differ from the reference program's by a relative error of at most 0.013.
Values may be sent and summed in bfloat16 or wider, within the bound.
No kernel may reach another device: no remote copies, remote signals or barrier semaphores. Data moves between devices by JAX's collectives and lax.ppermute only.
A program may use at most 128 MiB of HBM per device.

```python
import math
import jax
import jax.numpy as jnp
from jax import lax

SEG = 64
GROUP = 8
KMAX = 32
BLOCKS_DEV = 512
PARAMS = 2097152
BLOCKS = 4096
REPS = 32
N_FSDP = 8


def draw_bands(key, part):
    key = jax.random.fold_in(key, 11)
    scores = jax.random.randint(key, (REPS, BLOCKS, SEG), 0, 1 << 20) * SEG + jnp.arange(SEG, dtype=jnp.int32)
    picked = jax.lax.top_k(scores, KMAX)[1]
    return picked.astype(jnp.int32)


def draw_counts(key, part):
    key = jax.random.fold_in(key, 12)
    key_heavy, key_low, key_high, key_spot = jax.random.split(key, 4)
    holders = BLOCKS // BLOCKS_DEV
    heavy = jax.random.randint(key_heavy, (REPS, holders, 1), 0, 4) == 0
    heavy = jnp.broadcast_to(heavy, (REPS, holders, BLOCKS_DEV)).reshape(REPS, BLOCKS)
    low = jax.random.randint(key_low, (REPS, BLOCKS), 1, KMAX // 2 + 1)
    high = jax.random.randint(key_high, (REPS, BLOCKS), KMAX // 2, KMAX + 1)
    result = jnp.where(heavy, high, low)
    spot = jax.random.randint(key_spot, (REPS, 1), 0, BLOCKS)
    result = jnp.where(jnp.arange(BLOCKS, dtype=jnp.int32)[None, :] == spot, KMAX, result)
    return result.astype(jnp.int32)


def spiked(values, own_key, source, target, blocks, factor):
    def block_of(dim):
        return (jnp.arange(values.shape[dim]) // (values.shape[dim] // blocks)).reshape((-1,) + (1,) * (values.ndim - 1 - dim))

    first = jax.random.permutation(own_key, blocks)[block_of(target)]
    far = (block_of(target) + blocks // 2) % blocks
    return jnp.where((block_of(source) == first) | (block_of(source) == far), factor * values, values)


def shard_levels(own_key, extent, cuts, smallest, top_value):
    def one(dim, shards_of):
        draws = jax.random.uniform(jax.random.fold_in(jax.random.fold_in(own_key, 6), dim), (shards_of,), jnp.float32, smallest / len(cuts), top_value / len(cuts))
        return jnp.repeat(jnp.exp(draws), extent[dim] // shards_of).reshape((-1,) + (1,) * (len(extent) - dim - 1))

    factor_of = one(*cuts[0])
    for cut in cuts[1:]:
        factor_of = factor_of * one(*cut)
    return factor_of


def normal_values(own_key, dims, deviation, bound, cuts=(), kind=jnp.bfloat16):
    values = deviation * jax.random.normal(own_key, dims, jnp.float32)
    if cuts:
        values = values * shard_levels(own_key, dims, cuts, -0.22, 0.18)
    return jnp.clip(values, -bound, bound).astype(kind)


def noise_with(rng, dims, width, limit, shards, heavy, held_as=jnp.bfloat16):
    values = width * jax.random.normal(rng, dims, jnp.float32)
    if shards:
        values = values * shard_levels(rng, dims, shards, -0.22, 0.18)
    return jnp.clip(spiked(values, jax.random.fold_in(rng, 3), *heavy), -limit, limit).astype(held_as)


def setup_inputs(seed: int = 0) -> dict:
    streams_of = jax.random.split(jax.random.key(seed), 5)
    grad_parts = noise_with(streams_of[0], (REPS, N_FSDP, PARAMS), 0.5, 6.0, ((0, 32), (1, 8)), (1, 2, 8, 2.0))
    momentum = normal_values(streams_of[1], (REPS, PARAMS), 1.0, 6.0, ((0, 32), (1, 8)), jnp.float32)
    bands = draw_bands(jax.random.fold_in(streams_of[4], 71), 0)
    counts = draw_counts(jax.random.fold_in(streams_of[4], 71), 0)
    return dict(grad_parts=grad_parts, momentum=momentum, bands=bands, counts=counts)


HIGH = lax.Precision.HIGHEST

def cosine_table():
    freq = jnp.arange(SEG, dtype=jnp.int32)[:, None].astype(jnp.float32)
    point = jnp.arange(SEG, dtype=jnp.int32)[None, :].astype(jnp.float32)
    scale = jnp.where(freq == 0.0, jnp.float32(math.sqrt(1.0 / SEG)), jnp.float32(math.sqrt(2.0 / SEG)))
    return (scale * jnp.cos(jnp.float32(math.pi) * (2.0 * point + 1.0) * freq / (2.0 * SEG))).astype(jnp.float32)

def reference(grad_parts, momentum, bands, counts):
    table = cosine_table()
    freqs = jnp.arange(SEG, dtype=jnp.int32)
    slots = jnp.arange(KMAX, dtype=jnp.int32)

    def one_replica(total, index):
        parts = lax.dynamic_index_in_dim(grad_parts, index, 0, keepdims=False)
        grad = lax.optimization_barrier(jnp.sum(parts.astype(jnp.float32), axis=0))
        moment = 0.999 * lax.dynamic_index_in_dim(momentum, index, 0, keepdims=False) + grad
        rows = moment.reshape(BLOCKS, GROUP, SEG)
        coeff = jnp.einsum('cgn,kn->cgk', rows, table, precision=HIGH)
        lists = lax.dynamic_index_in_dim(bands, index, 0, keepdims=False)
        live = lax.dynamic_index_in_dim(counts, index, 0, keepdims=False)
        onehot = ((lists[:, :, None] == freqs[None, None, :]) & (slots[None, :, None] < live[:, None, None])).astype(jnp.float32)
        values = jnp.einsum('cgf,ckf->cgk', coeff, onehot, precision=HIGH).astype(jnp.bfloat16)
        sent = jnp.einsum('cgk,ckf->cgf', values.astype(jnp.float32), onehot, precision=HIGH)
        back = jnp.einsum('cgf,fn->cgn', sent, table, precision=HIGH)
        return (total + sent, moment - back.reshape(-1))
    start = jnp.zeros((BLOCKS, GROUP, SEG), jnp.float32)
    total, new_momentum = lax.scan(one_replica, start, jnp.arange(REPS, dtype=jnp.int32))
    update = jnp.einsum('cgf,fn->cgn', total, table, precision=HIGH).reshape(-1) / jnp.float32(math.sqrt(REPS))
    return (new_momentum, update)
```

```python
import math

import jax
import jax.numpy as jnp
import numpy as np
from jax import lax
from jax.experimental import pallas as pl
from jax.experimental.pallas import tpu as pltpu
from jax.sharding import PartitionSpec as P

SEG = 64
GROUP = 8
KMAX = 32
LANES = 128

HIGH = lax.Precision.HIGHEST
BF16 = jnp.bfloat16
F32 = jnp.float32


def paired_table():
    freq = np.arange(SEG, dtype=np.float64)[:, None]
    point = np.arange(SEG, dtype=np.float64)[None, :]
    scale = np.where(freq == 0.0, math.sqrt(1.0 / SEG), math.sqrt(2.0 / SEG))
    table = scale * np.cos(math.pi * (2.0 * point + 1.0) * freq / (2.0 * SEG))
    return np.kron(np.eye(2), table).astype(np.float32)


def unpack_pieces(raw, order):
    count = order.shape[0]
    size = raw.shape[-1] // 8
    rows = size // LANES
    step = min(rows, 128)

    def kernel(order_ref, raw_ref, *refs):
        outs, (held, dense, sem_in, sem_out) = refs[:count], refs[count:]

        def fetch(i):
            at = pl.multiple_of(order_ref[i] * size, size)
            return pltpu.make_async_copy(
                raw_ref.at[:, :, pl.ds(at, size)], held.at[i], sem_in.at[i]
            )

        def store(i):
            return pltpu.make_async_copy(dense.at[i], outs[i], sem_out.at[i])

        for i in range(count):
            fetch(i).start()
        for i in range(count):
            fetch(i).wait()

            @pl.loop(0, rows // step)
            def _(j):
                some = held[i, 0, :, pl.ds(pl.multiple_of(j * step * LANES, step * LANES), step * LANES)]
                dense[i, pl.ds(pl.multiple_of(j * step, step), step), :] = some.reshape(step, LANES)

            store(i).start()
        for i in range(count):
            store(i).wait()

    return pl.pallas_call(
        kernel,
        in_specs=[pl.BlockSpec(memory_space=pltpu.SMEM), pl.BlockSpec(memory_space=pl.ANY)],
        out_specs=[pl.BlockSpec(memory_space=pl.ANY)] * count,
        out_shape=[jax.ShapeDtypeStruct((rows, LANES), BF16)] * count,
        scratch_shapes=[
            pltpu.VMEM((count, 1, 1, size), BF16),
            pltpu.VMEM((count, rows, LANES), BF16),
            pltpu.SemaphoreType.DMA((count,)),
            pltpu.SemaphoreType.DMA((count,)),
        ],
        compiler_params=pltpu.CompilerParams(vmem_limit_bytes=24 << 20),
        cost_estimate=pl.CostEstimate(flops=0, bytes_accessed=count * size * 6, transcendentals=0),
    )(order, raw)


def transform_step(terms, momentum, mask, paired):
    rows = momentum.shape[0]
    step = min(rows, 512)

    def kernel(*refs):
        parts, (mom_ref, mask_ref, fwd_ref, inv_ref, sent_ref, new_ref) = refs[:-6], refs[-6:]
        grad = parts[0][...].astype(F32)
        for part in parts[1:]:
            grad = grad + part[...].astype(F32)
        moment = 0.999 * mom_ref[...] + grad
        coeff = jnp.dot(moment, fwd_ref[...], precision=HIGH, preferred_element_type=F32)
        sent = jnp.where(mask_ref[...].astype(F32) > 0.5, coeff, 0.0).astype(BF16)
        sent_ref[...] = sent
        back = jnp.dot(sent.astype(F32), inv_ref[...], precision=HIGH, preferred_element_type=F32)
        new_ref[...] = moment - back

    block = pl.BlockSpec((step, LANES), lambda i: (i, 0))
    whole = pl.BlockSpec((LANES, LANES), lambda i: (0, 0))
    return pl.pallas_call(
        kernel,
        grid=(rows // step,),
        in_specs=[block] * (len(terms) + 2) + [whole] * 2,
        out_specs=[block] * 2,
        out_shape=[
            jax.ShapeDtypeStruct((rows, LANES), BF16),
            jax.ShapeDtypeStruct((rows, LANES), F32),
        ],
        compiler_params=pltpu.CompilerParams(vmem_limit_bytes=24 << 20),
        cost_estimate=pl.CostEstimate(
            flops=rows * LANES * LANES * 24, bytes_accessed=rows * LANES * 24, transcendentals=0
        ),
    )(*terms, momentum, mask, jnp.asarray(paired.T), jnp.asarray(paired))


def combine_step(pieces, paired, factor):
    count, rows, _ = pieces.shape

    def kernel(pieces_ref, inv_ref, out_ref):
        total = jnp.sum(pieces_ref[...].astype(F32), axis=0)
        back = jnp.dot(total, inv_ref[...], precision=HIGH, preferred_element_type=F32)
        out_ref[...] = jnp.broadcast_to((back * factor).astype(BF16)[None], out_ref.shape)

    return pl.pallas_call(
        kernel,
        out_shape=jax.ShapeDtypeStruct(pieces.shape, BF16),
        compiler_params=pltpu.CompilerParams(vmem_limit_bytes=24 << 20),
        cost_estimate=pl.CostEstimate(
            flops=pieces.size, bytes_accessed=pieces.size * 4, transcendentals=0
        ),
    )(pieces, jnp.asarray(paired))


def body(grad_parts, momentum, bands, counts):
    replicas = lax.axis_size("rep")
    holders = lax.axis_size("fsdp")
    chips = holders // 2
    me = lax.axis_index("fsdp")
    core = me % 2
    chip = me // 2
    paired = paired_table()

    blocks = momentum.size // (GROUP * SEG)
    rows = momentum.size // LANES

    ahead = (chip + jnp.array([1, 2, 3, 0], jnp.int32)) % chips
    theirs = unpack_pieces(grad_parts, 2 * ahead + (1 - core))
    mine = unpack_pieces(grad_parts, 2 * ahead + core)
    swap = [(f, f ^ 1) for f in range(holders)]
    given = [lax.ppermute(t, "fsdp", swap) for t in theirs]

    def hop(n):
        return [(2 * c + k, 2 * ((c + n) % chips) + k) for c in range(chips) for k in range(2)]

    terms = [mine[3], given[3]]
    for i, n in enumerate((1, 2, 3)):
        both = (mine[i].astype(F32) + given[i].astype(F32)).astype(BF16)
        terms.append(lax.ppermute(both, "fsdp", hop(n)))

    freqs = jnp.arange(SEG, dtype=jnp.int32)
    slots = jnp.arange(KMAX, dtype=jnp.int32)
    lists = bands.reshape(blocks, KMAX)
    live = counts.reshape(blocks)
    hot = jnp.any(
        (lists[:, :, None] == freqs[None, None, :]) & (slots[None, :, None] < live[:, None, None]),
        axis=1,
    ).astype(BF16)
    mask = jnp.broadcast_to(
        jnp.concatenate([hot, hot], axis=1)[:, None, :], (blocks, GROUP // 2, LANES)
    ).reshape(rows, LANES)

    sent, new = transform_step(terms, momentum.reshape(rows, LANES), mask, paired)
    each = lax.all_to_all(
        sent.reshape(replicas, rows // replicas, LANES), "rep", split_axis=0, concat_axis=0, tiled=True
    )
    mixed = combine_step(each, paired, 1.0 / math.sqrt(replicas))
    update = lax.all_to_all(mixed, "rep", split_axis=0, concat_axis=0, tiled=True)
    return (new.reshape(momentum.shape), update.astype(F32).reshape(-1))


def solution(mesh):
    placed = (P("rep", "fsdp", None), P("rep", "fsdp"), P("rep", "fsdp", None), P("rep", "fsdp"))
    return jax.shard_map(
        body, mesh=mesh, in_specs=placed, out_specs=(P("rep", "fsdp"), P("fsdp")), check_vma=False
    )
```

```python
import math

import jax
import jax.numpy as jnp
import numpy as np
from jax import lax
from jax.experimental import pallas as pl
from jax.experimental.pallas import tpu as pltpu
from jax.sharding import PartitionSpec as P

SEG = 64
GROUP = 8
KMAX = 32
LANES = 128
CORES = 2
PIECES = 8
VMEM_LIMIT = 20 << 20

BF16 = jnp.bfloat16
F32 = jnp.float32
VMEM = pl.BlockSpec(memory_space=pltpu.VMEM)


def paired_table():
    freq = np.arange(SEG, dtype=np.float64)[:, None]
    point = np.arange(SEG, dtype=np.float64)[None, :]
    scale = np.where(freq == 0.0, math.sqrt(1.0 / SEG), math.sqrt(2.0 / SEG))
    table = scale * np.cos(math.pi * (2.0 * point + 1.0) * freq / (2.0 * SEG))
    paired = np.kron(np.eye(2), table).astype(np.float32)
    high = paired.astype(BF16)
    low = (paired - high.astype(np.float32)).astype(BF16)
    return high, low


def forward_table():
    high, low = paired_table()
    return np.block([[high.T, low.T], [high.T, np.zeros_like(low)]]).astype(BF16)


def inverse_table():
    high, low = paired_table()
    return np.block([[high, low], [high, np.zeros_like(low)]]).astype(BF16)


def split(x):
    high = x.astype(BF16)
    low = (x - high.astype(F32)).astype(BF16)
    return jnp.concatenate([high, low], axis=1)


def product(x, table):
    out = jnp.dot(x, table, preferred_element_type=F32)
    return out[:, :LANES] + out[:, LANES:]


def unpack(raw, wanted):
    count = len(wanted)
    size = raw.shape[-1] // PIECES
    rows = size // LANES
    cuts = 2
    cut = size // cuts
    lines = cut // LANES
    step = min(lines, 128)

    def kernel(raw_ref, *refs):
        outs, (held, sems) = refs[:count], refs[count:]
        me = lax.axis_index("fsdp")
        chip, core = me // CORES, lax.rem(me, CORES)

        def fetch(i, j):
            n, other = wanted[i]
            lane = lax.rem(core + other, CORES)
            to = (chip, chip + 1 - 2 * lax.rem(chip, 2), lax.rem(chip + 2, 4), 3 - chip)[n]
            piece = to * CORES + lane
            at = pl.multiple_of(piece * size + j * cut, cut)
            return pltpu.make_async_copy(
                raw_ref.at[:, :, pl.ds(at, cut)], held.at[i * cuts + j], sems.at[i * cuts + j]
            )

        for i in range(count):
            for j in range(cuts):
                fetch(i, j).start()
        for i in range(count):
            for j in range(cuts):
                fetch(i, j).wait()
                for k in range(lines // step):
                    some = held[i * cuts + j, 0, :, pl.ds(k * step * LANES, step * LANES)]
                    outs[i][pl.ds(j * lines + k * step, step), :] = some.reshape(step, LANES)

    return pl.pallas_call(
        kernel,
        in_specs=[pl.BlockSpec(memory_space=pltpu.HBM)],
        out_specs=[VMEM] * count,
        out_shape=[jax.ShapeDtypeStruct((rows, LANES), BF16)] * count,
        scratch_shapes=[
            pltpu.VMEM((count * cuts, 1, 1, cut), BF16),
            pltpu.SemaphoreType.DMA((count * cuts,)),
        ],
        compiler_params=pltpu.CompilerParams(vmem_limit_bytes=VMEM_LIMIT),
        cost_estimate=pl.CostEstimate(flops=0, bytes_accessed=count * size * 6, transcendentals=0),
    )(raw)


def local_kernel(kernel, shapes, *args):
    return pl.pallas_call(
        kernel,
        in_specs=[VMEM] * len(args),
        out_specs=[VMEM] * len(shapes),
        out_shape=[jax.ShapeDtypeStruct(s, t) for s, t in shapes],
        compiler_params=pltpu.CompilerParams(vmem_limit_bytes=VMEM_LIMIT),
        cost_estimate=pl.CostEstimate(
            flops=0, bytes_accessed=sum(a.size * a.dtype.itemsize for a in args), transcendentals=0
        ),
    )(*args)


def far_kernel(mine_ref, given_ref, low_ref, high_ref):
    half = low_ref.shape[0]
    for at, out in ((0, low_ref), (half, high_ref)):
        some = pl.ds(at, half)
        out[...] = (mine_ref[some, :].astype(F32) + given_ref[some, :].astype(F32)).astype(BF16)


def near_kernel(mine1_ref, given1_ref, mine3_ref, given3_ref, near1_ref, near3_ref, sum1_ref, sum3_ref):
    half = near1_ref.shape[0]
    low, high = pl.ds(0, half), pl.ds(half, half)
    near1_ref[...] = (mine1_ref[low, :].astype(F32) + given1_ref[low, :].astype(F32)).astype(BF16)
    near3_ref[...] = (mine3_ref[high, :].astype(F32) + given3_ref[high, :].astype(F32)).astype(BF16)
    sum1_ref[...] = mine1_ref[high, :].astype(F32) + given1_ref[high, :].astype(F32)
    sum3_ref[...] = mine3_ref[low, :].astype(F32) + given3_ref[low, :].astype(F32)


def last_kernel(sum_ref, far_ref, out_ref):
    out_ref[...] = (sum_ref[...] + far_ref[...].astype(F32)).astype(BF16)


def base_kernel(mom_ref, mine_ref, given_ref, low_ref, high_ref, hot_ref, fwd_ref, inv_ref, out_ref, mask_ref):
    half = low_ref.shape[0]
    for at, part in ((0, low_ref), (half, high_ref)):
        some = pl.ds(at, half)
        out_ref[some, :] = (
            0.999 * mom_ref[some, :]
            + mine_ref[some, :].astype(F32)
            + given_ref[some, :].astype(F32)
            + part[...].astype(F32)
        )
    blocks = hot_ref.shape[0]
    hot = hot_ref[...].astype(F32)
    for q in range(GROUP // 2):
        mask_ref[pl.ds(q, blocks, stride=GROUP // 2), :] = hot


def guess_kernel(base_ref, fwd_ref, coeff_ref):
    rows = base_ref.shape[0]
    step = min(rows, 256)
    for k in range(rows // step):
        some = pl.ds(k * step, step)
        coeff_ref[some, :] = product(split(base_ref[some, :]), fwd_ref[...])


def keep_kernel(coeff_ref, low_ref, high_ref, mask_ref, fwd_ref, sent_ref):
    half = low_ref.shape[0]
    step = min(half, 256)
    for at, part in ((0, low_ref), (half, high_ref)):
        for k in range(half // step):
            some = pl.ds(at + k * step, step)
            coeff = coeff_ref[some, :] + product(part[pl.ds(k * step, step), :], fwd_ref[:LANES, :])
            sent_ref[some, :] = jnp.where(mask_ref[some, :] > 0.5, coeff, 0.0).astype(BF16)


def remove_kernel(sent_ref, base_ref, low_ref, high_ref, inv_ref, new_ref):
    half = low_ref.shape[0]
    step = min(half, 256)
    for at, part in ((0, low_ref), (half, high_ref)):
        for k in range(half // step):
            some = pl.ds(at + k * step, step)
            moment = base_ref[some, :] + part[pl.ds(k * step, step), :].astype(F32)
            new_ref[some, :] = moment - product(sent_ref[some, :], inv_ref[:LANES, :])


def combine_kernel(factor, pieces_ref, inv_ref, out_ref):
    total = jnp.sum(pieces_ref[...].astype(F32), axis=0)
    back = product(split(total), inv_ref[...]) * factor
    out_ref[...] = jnp.broadcast_to(back.astype(BF16)[None], out_ref.shape)


def spread_kernel(zs, *refs):
    planes, out_ref = refs[:-1], refs[-1]
    count = planes[0].shape[0]
    x = lax.axis_index("rep") // zs
    order = (x, x + 1 - 2 * lax.rem(x, 2), lax.rem(x + 2, 4), 3 - x)
    for n, ref in enumerate(planes):
        out_ref[pl.ds(pl.multiple_of(order[n] * count, count), count), :] = ref[...].astype(F32)


def body(grad_parts, momentum, bands, counts):
    replicas = lax.axis_size("rep")
    holders = lax.axis_size("fsdp")
    forward, inverse = jnp.asarray(forward_table()), jnp.asarray(inverse_table())

    blocks = momentum.size // (GROUP * SEG)
    rows = momentum.size // LANES
    half = rows // 2

    freqs = jnp.arange(SEG, dtype=jnp.int32)
    slots = jnp.arange(KMAX, dtype=jnp.int32)
    lists = bands.reshape(blocks, KMAX)
    live = counts.reshape(blocks)
    hot = jnp.any(
        (lists[:, :, None] == freqs[None, None, :]) & (slots[None, :, None] < live[:, None, None]),
        axis=1,
    ).astype(BF16)
    hot = jnp.concatenate([hot, hot], axis=1)

    whole, part = (rows, LANES), (half, LANES)

    def over_cores(x):
        return lax.ppermute(x, "fsdp", [(f, f ^ 1) for f in range(holders)])

    def trade(x, n):
        return lax.ppermute(x, "fsdp", [(f, f ^ (CORES * n)) for f in range(holders)])

    (theirs2,) = unpack(grad_parts, ((2, 1),))
    given2 = over_cores(theirs2)
    mine2, theirs1, theirs3, mine1, mine3, theirs0, mine0 = unpack(
        grad_parts, ((2, 0), (1, 1), (3, 1), (1, 0), (3, 0), (0, 1), (0, 0))
    )
    given1, given3 = over_cores(theirs1), over_cores(theirs3)
    far1, far3 = local_kernel(far_kernel, [(part, BF16)] * 2, mine2, given2)
    far1, far3 = trade(far1, 1), trade(far3, 3)
    given0 = over_cores(theirs0)
    near1, near3, sum1, sum3 = local_kernel(
        near_kernel, [(part, BF16)] * 2 + [(part, F32)] * 2, mine1, given1, mine3, given3
    )
    near_low, near_high = trade(near1, 1), trade(near3, 3)
    (last3,) = local_kernel(last_kernel, [(part, BF16)], sum3, far1)
    last_low = trade(last3, 3)
    (last1,) = local_kernel(last_kernel, [(part, BF16)], sum1, far3)
    last_high = trade(last1, 1)

    base, mask = local_kernel(
        base_kernel,
        [(whole, F32)] * 2,
        momentum.reshape(whole),
        mine0,
        given0,
        near_low,
        near_high,
        hot,
        forward,
        inverse,
    )
    (coeff,) = local_kernel(guess_kernel, [(whole, F32)], base, forward)
    (sent,) = local_kernel(keep_kernel, [(whole, BF16)], coeff, last_low, last_high, mask, forward)
    (new,) = local_kernel(remove_kernel, [(whole, F32)], sent, base, last_low, last_high, inverse)

    pieces = lax.all_to_all(
        sent.reshape(replicas, rows // replicas, LANES), "rep", split_axis=0, concat_axis=0, tiled=True
    )
    xs = 4
    zs = replicas // xs
    (mixed,) = local_kernel(
        lambda *refs: combine_kernel(1.0 / math.sqrt(replicas), *refs),
        [((zs,) + pieces.shape[1:], BF16)],
        pieces,
        inverse,
    )
    lines = [[zs * x + z for z in range(zs)] for x in range(xs)]
    plane = lax.all_to_all(
        mixed, "rep", split_axis=0, concat_axis=0, axis_index_groups=lines, tiled=True
    ).reshape(rows // xs, LANES)

    def across(n):
        return lax.ppermute(plane, "rep", [(r, r ^ (zs * n)) for r in range(replicas)])

    planes = [plane] + [across(n) for n in (1, 2, 3)]
    (update,) = local_kernel(lambda *refs: spread_kernel(zs, *refs), [(whole, F32)], *planes)
    return (new.reshape(momentum.shape), update.reshape(-1))


def solution(mesh):
    placed = (P("rep", "fsdp", None), P("rep", "fsdp"), P("rep", "fsdp", None), P("rep", "fsdp"))
    return jax.shard_map(
        body, mesh=mesh, in_specs=placed, out_specs=(P("rep", "fsdp"), P("fsdp")), check_vma=False
    )
```

```python
import math

import jax
import jax.numpy as jnp
import numpy as np
from jax import lax
from jax.experimental import pallas as pl
from jax.experimental.pallas import tpu as pltpu
from jax.sharding import PartitionSpec as P

SEG = 64
GROUP = 8
KMAX = 32
LANES = 128
CORES = 2
PIECES = 8
VMEM_LIMIT = 20 << 20
SUB = 8
QUADS = GROUP // 2

BF16 = jnp.bfloat16
F32 = jnp.float32
VMEM = pl.BlockSpec(memory_space=pltpu.VMEM)


def paired_table():
    freq = np.arange(SEG, dtype=np.float64)[:, None]
    point = np.arange(SEG, dtype=np.float64)[None, :]
    scale = np.where(freq == 0.0, math.sqrt(1.0 / SEG), math.sqrt(2.0 / SEG))
    table = scale * np.cos(math.pi * (2.0 * point + 1.0) * freq / (2.0 * SEG))
    paired = np.kron(np.eye(2), table).astype(np.float32)
    high = paired.astype(BF16)
    low = (paired - high.astype(np.float32)).astype(BF16)
    return high, low


def forward_table():
    high, low = paired_table()
    return np.block([[high.T, low.T], [high.T, np.zeros_like(low)]]).astype(BF16)


def inverse_table():
    high, low = paired_table()
    return np.block([[high, low], [high, np.zeros_like(low)]]).astype(BF16)


def split(x):
    high = x.astype(BF16)
    low = (x - high.astype(F32)).astype(BF16)
    return jnp.concatenate([high, low], axis=1)


def product(x, table):
    out = jnp.dot(x, table, preferred_element_type=F32)
    return out[:, :LANES] + out[:, LANES:]


def unpack(raw, wanted):
    count = len(wanted)
    size = raw.shape[-1] // PIECES
    rows = size // LANES
    cuts = 2
    cut = size // cuts
    lines = cut // LANES
    step = min(lines, 128)

    def kernel(raw_ref, *refs):
        outs, (held, sems) = refs[:count], refs[count:]
        me = lax.axis_index("fsdp")
        chip, core = me // CORES, lax.rem(me, CORES)

        def fetch(i, j):
            n, other = wanted[i]
            lane = lax.rem(core + other, CORES)
            to = (chip, chip + 1 - 2 * lax.rem(chip, 2), lax.rem(chip + 2, 4), 3 - chip)[n]
            piece = to * CORES + lane
            at = pl.multiple_of(piece * size + j * cut, cut)
            return pltpu.make_async_copy(
                raw_ref.at[:, :, pl.ds(at, cut)], held.at[i * cuts + j], sems.at[i * cuts + j]
            )

        for i in range(count):
            for j in range(cuts):
                fetch(i, j).start()
        for i in range(count):
            for j in range(cuts):
                fetch(i, j).wait()
                for k in range(lines // step):
                    some = held[i * cuts + j, 0, :, pl.ds(k * step * LANES, step * LANES)]
                    outs[i][pl.ds(j * lines + k * step, step), :] = some.reshape(step, LANES)

    return pl.pallas_call(
        kernel,
        in_specs=[pl.BlockSpec(memory_space=pltpu.HBM)],
        out_specs=[VMEM] * count,
        out_shape=[jax.ShapeDtypeStruct((rows, LANES), BF16)] * count,
        scratch_shapes=[
            pltpu.VMEM((count * cuts, 1, 1, cut), BF16),
            pltpu.SemaphoreType.DMA((count * cuts,)),
        ],
        compiler_params=pltpu.CompilerParams(vmem_limit_bytes=VMEM_LIMIT),
        cost_estimate=pl.CostEstimate(flops=0, bytes_accessed=count * size * 6, transcendentals=0),
    )(raw)


def local_kernel(kernel, shapes, *args, scratch=()):
    return pl.pallas_call(
        kernel,
        in_specs=[VMEM] * len(args),
        out_specs=[VMEM] * len(shapes),
        out_shape=[jax.ShapeDtypeStruct(s, t) for s, t in shapes],
        scratch_shapes=[pltpu.VMEM(s, t) for s, t in scratch],
        compiler_params=pltpu.CompilerParams(vmem_limit_bytes=VMEM_LIMIT),
        cost_estimate=pl.CostEstimate(
            flops=0, bytes_accessed=sum(a.size * a.dtype.itemsize for a in args), transcendentals=0
        ),
    )(*args)


def far_kernel(mine_ref, given_ref, low_ref, high_ref):
    half = low_ref.shape[0]
    for at, out in ((0, low_ref), (half, high_ref)):
        some = pl.ds(at, half)
        out[...] = (mine_ref[some, :].astype(F32) + given_ref[some, :].astype(F32)).astype(BF16)


def near_kernel(mine1_ref, given1_ref, mine3_ref, given3_ref, near1_ref, near3_ref, sum1_ref, sum3_ref):
    half = near1_ref.shape[0]
    low, high = pl.ds(0, half), pl.ds(half, half)
    near1_ref[...] = (mine1_ref[low, :].astype(F32) + given1_ref[low, :].astype(F32)).astype(BF16)
    near3_ref[...] = (mine3_ref[high, :].astype(F32) + given3_ref[high, :].astype(F32)).astype(BF16)
    sum1_ref[...] = mine1_ref[high, :].astype(F32) + given1_ref[high, :].astype(F32)
    sum3_ref[...] = mine3_ref[low, :].astype(F32) + given3_ref[low, :].astype(F32)


def last_kernel(sum_ref, far_ref, out_ref):
    out_ref[...] = (sum_ref[...] + far_ref[...].astype(F32)).astype(BF16)


def list_kernel(bands_ref, counts_ref, _, hot_ref, ranks_ref, pick_ref):
    blocks = bands_ref.shape[1]
    for k in range(blocks // LANES):
        some = pl.ds(k * LANES, LANES)
        slots = lax.broadcasted_iota(jnp.int32, (KMAX, LANES), 0)
        place = jnp.where(slots < counts_ref[:, some], bands_ref[:, some], -LANES)
        freqs = lax.broadcasted_iota(jnp.int32, (SEG, LANES), 0)
        rank = jnp.zeros((SEG, LANES), jnp.int32)
        for j in range(KMAX):
            rank = jnp.where(freqs == place[j : j + 1], j + 1, rank)
        rank = rank.astype(F32)
        rank = jnp.concatenate([rank, rank], axis=0).T
        place = place.astype(F32)
        place = jnp.concatenate([place, place + SEG, place, place + SEG], axis=0).T
        hot_ref[some, :] = rank
        first = lax.broadcasted_iota(jnp.int32, (SUB, LANES), 1) < SEG
        for p in range(LANES // (2 * SUB)):
            at = p * 2 * SUB
            out = pl.ds(k * (LANES // 2) + p * SUB, SUB)
            ranks_ref[out, :] = jnp.where(first, rank[at : at + SUB], rank[at + SUB : at + 2 * SUB])
            both = jnp.where(first, place[at : at + SUB], place[at + SUB : at + 2 * SUB])
            pick_ref[out, :] = both.astype(jnp.int32)


def base_kernel(mom_ref, mine_ref, given_ref, low_ref, high_ref, hot_ref, fwd_ref, inv_ref, out_ref, mask_ref):
    half = low_ref.shape[0]
    for at, part in ((0, low_ref), (half, high_ref)):
        some = pl.ds(at, half)
        out_ref[some, :] = (
            0.999 * mom_ref[some, :]
            + mine_ref[some, :].astype(F32)
            + given_ref[some, :].astype(F32)
            + part[...].astype(F32)
        )
    blocks = hot_ref.shape[0]
    hot = hot_ref[...].astype(F32)
    for q in range(QUADS):
        mask_ref[pl.ds(q, blocks, stride=QUADS), :] = hot


def guess_kernel(base_ref, fwd_ref, coeff_ref):
    rows = base_ref.shape[0]
    step = min(rows, 256)
    for k in range(rows // step):
        some = pl.ds(k * step, step)
        coeff_ref[some, :] = product(split(base_ref[some, :]), fwd_ref[...])


def lane_gather(x, index):
    return jnp.take_along_axis(x, index, axis=1, mode="promise_in_bounds")


def keep_kernel(coeff_ref, low_ref, high_ref, mask_ref, pick_ref, rank_ref, fwd_ref, sent_ref, pack_ref, held_ref):
    half = low_ref.shape[0]
    piece = 2 * SUB * QUADS
    step = min(half, 256)
    first = lax.broadcasted_iota(jnp.int32, (SUB, LANES), 1) < SEG
    for at, part in ((0, low_ref), (half, high_ref)):
        for k in range(half // step):
            start = at + k * step
            some = pl.ds(start, step)
            coeff = coeff_ref[some, :] + product(part[pl.ds(k * step, step), :], fwd_ref[:LANES, :])
            held_ref[some, :] = coeff
            sent_ref[some, :] = jnp.where(mask_ref[some, :] > 0.5, coeff, 0.0).astype(BF16)
            for p in range(start // piece, (start + step) // piece):
                pick = pick_ref[pl.ds(p * SUB, SUB), :]
                index = jnp.maximum(pick, 0)
                out = []
                for q in range(QUADS):
                    one = held_ref[pl.ds(p * piece + q, SUB, stride=QUADS), :]
                    two = held_ref[pl.ds(p * piece + piece // 2 + q, SUB, stride=QUADS), :]
                    both = jnp.where(first, lane_gather(one, index), lane_gather(two, index))
                    out.append(jnp.where(pick >= 0, both, 0.0))
                out.append(rank_ref[pl.ds(p * SUB, SUB), :])
                pack_ref[p] = jnp.concatenate(out, axis=0).astype(BF16)


def remove_kernel(sent_ref, base_ref, low_ref, high_ref, inv_ref, new_ref):
    half = low_ref.shape[0]
    step = min(half, 256)
    for at, part in ((0, low_ref), (half, high_ref)):
        for k in range(half // step):
            some = pl.ds(at + k * step, step)
            moment = base_ref[some, :] + part[pl.ds(k * step, step), :].astype(F32)
            new_ref[some, :] = moment - product(sent_ref[some, :], inv_ref[:LANES, :])


def combine_kernel(factor, pieces_ref, inv_ref, out_ref, held_ref):
    first = lax.broadcasted_iota(jnp.int32, (SUB, LANES), 1) < SEG
    shift = jnp.where(first, -1, KMAX - 1)
    totals = [jnp.zeros((SUB, LANES), F32) for _ in range(2 * QUADS)]
    for r in range(pieces_ref.shape[0]):
        piece = pieces_ref[r].astype(F32)
        rank = piece[SUB * QUADS :]
        other = pltpu.roll(rank, SEG, axis=1)
        for h in range(2):
            place = jnp.where(first, rank, other) if h == 0 else jnp.where(first, other, rank)
            index = jnp.maximum(place.astype(jnp.int32) + shift, 0) + h * SEG
            for q in range(QUADS):
                value = lane_gather(piece[q * SUB : (q + 1) * SUB], index)
                totals[h * QUADS + q] += jnp.where(place > 0.5, value, 0.0)
    back = product(split(jnp.concatenate(totals, axis=0)), inv_ref[...]) * factor
    for h in range(2):
        for q in range(QUADS):
            at = (h * QUADS + q) * SUB
            held_ref[pl.ds(h * SUB * QUADS + q, SUB, stride=QUADS), :] = back[at : at + SUB]
    out_ref[...] = jnp.broadcast_to(held_ref[...].astype(BF16)[None], out_ref.shape)


def spread_kernel(zs, *refs):
    planes, out_ref = refs[:-1], refs[-1]
    count = planes[0].shape[0]
    x = lax.axis_index("rep") // zs
    order = (x, x + 1 - 2 * lax.rem(x, 2), lax.rem(x + 2, 4), 3 - x)
    for n, ref in enumerate(planes):
        out_ref[pl.ds(pl.multiple_of(order[n] * count, count), count), :] = ref[...].astype(F32)


def body(grad_parts, momentum, bands, counts):
    replicas = lax.axis_size("rep")
    holders = lax.axis_size("fsdp")
    forward, inverse = jnp.asarray(forward_table()), jnp.asarray(inverse_table())

    blocks = momentum.size // (GROUP * SEG)
    rows = momentum.size // LANES
    half = rows // 2

    whole, part = (rows, LANES), (half, LANES)

    def over_cores(x):
        return lax.ppermute(x, "fsdp", [(f, f ^ 1) for f in range(holders)])

    def trade(x, n):
        return lax.ppermute(x, "fsdp", [(f, f ^ (CORES * n)) for f in range(holders)])

    (theirs2,) = unpack(grad_parts, ((2, 1),))
    given2 = over_cores(theirs2)
    mine2, theirs1, theirs3, mine1, mine3, theirs0, mine0 = unpack(
        grad_parts, ((2, 0), (1, 1), (3, 1), (1, 0), (3, 0), (0, 1), (0, 0))
    )
    given1, given3 = over_cores(theirs1), over_cores(theirs3)
    far1, far3 = local_kernel(far_kernel, [(part, BF16)] * 2, mine2, given2)
    far1, far3 = trade(far1, 1), trade(far3, 3)
    given0 = over_cores(theirs0)
    near1, near3, sum1, sum3 = local_kernel(
        near_kernel, [(part, BF16)] * 2 + [(part, F32)] * 2, mine1, given1, mine3, given3
    )
    near_low, near_high = trade(near1, 1), trade(near3, 3)
    (last3,) = local_kernel(last_kernel, [(part, BF16)], sum3, far1)
    last_low = trade(last3, 3)
    (last1,) = local_kernel(last_kernel, [(part, BF16)], sum1, far3)
    last_high = trade(last1, 1)

    hot, ranks, pick = pl.pallas_call(
        list_kernel,
        in_specs=[VMEM, VMEM, pl.BlockSpec(memory_space=pl.ANY)],
        out_specs=[VMEM] * 3,
        out_shape=[
            jax.ShapeDtypeStruct((blocks, LANES), F32),
            jax.ShapeDtypeStruct((blocks // 2, LANES), F32),
            jax.ShapeDtypeStruct((blocks // 2, LANES), jnp.int32),
        ],
        compiler_params=pltpu.CompilerParams(vmem_limit_bytes=VMEM_LIMIT),
    )(bands.reshape(blocks, KMAX).T, counts, near_low)

    base, mask = local_kernel(
        base_kernel,
        [(whole, F32)] * 2,
        momentum.reshape(whole),
        mine0,
        given0,
        near_low,
        near_high,
        hot,
        forward,
        inverse,
    )
    (coeff,) = local_kernel(guess_kernel, [(whole, F32)], base, forward)
    sent, pack = local_kernel(
        keep_kernel,
        [(whole, BF16), ((replicas, SUB * (QUADS + 1), LANES), BF16)],
        coeff,
        last_low,
        last_high,
        mask,
        pick,
        ranks,
        forward,
        scratch=[(whole, F32)],
    )
    (new,) = local_kernel(remove_kernel, [(whole, F32)], sent, base, last_low, last_high, inverse)

    pieces = lax.all_to_all(pack, "rep", split_axis=0, concat_axis=0, tiled=True)
    xs = 4
    zs = replicas // xs
    (mixed,) = local_kernel(
        lambda *refs: combine_kernel(1.0 / math.sqrt(replicas), *refs),
        [((zs, 2 * SUB * QUADS, LANES), BF16)],
        pieces,
        inverse,
        scratch=[((2 * SUB * QUADS, LANES), F32)],
    )
    lines = [[zs * x + z for z in range(zs)] for x in range(xs)]
    plane = lax.all_to_all(
        mixed, "rep", split_axis=0, concat_axis=0, axis_index_groups=lines, tiled=True
    ).reshape(rows // xs, LANES)

    def across(n):
        return lax.ppermute(plane, "rep", [(r, r ^ (zs * n)) for r in range(replicas)])

    planes = [plane] + [across(n) for n in (1, 2, 3)]
    (update,) = local_kernel(lambda *refs: spread_kernel(zs, *refs), [(whole, F32)], *planes)
    return (new.reshape(momentum.shape), update.reshape(-1))


def solution(mesh):
    placed = (P("rep", "fsdp", None), P("rep", "fsdp"), P("rep", "fsdp", None), P("rep", "fsdp"))
    return jax.shard_map(
        body, mesh=mesh, in_specs=placed, out_specs=(P("rep", "fsdp"), P("fsdp")), check_vma=False
    )
```

```python
import math

import jax
import jax.numpy as jnp
import numpy as np
from jax import lax
from jax.experimental import pallas as pl
from jax.experimental.pallas import tpu as pltpu
from jax.sharding import PartitionSpec as P

SEG = 64
GROUP = 8
KMAX = 32
LANES = 128
CORES = 2
PIECES = 8
VMEM_LIMIT = 20 << 20
SUB = 8
QUADS = GROUP // 2

BF16 = jnp.bfloat16
F32 = jnp.float32
VMEM = pl.BlockSpec(memory_space=pltpu.VMEM)


def paired_table():
    freq = np.arange(SEG, dtype=np.float64)[:, None]
    point = np.arange(SEG, dtype=np.float64)[None, :]
    scale = np.where(freq == 0.0, math.sqrt(1.0 / SEG), math.sqrt(2.0 / SEG))
    table = scale * np.cos(math.pi * (2.0 * point + 1.0) * freq / (2.0 * SEG))
    paired = np.kron(np.eye(2), table).astype(np.float32)
    high = paired.astype(BF16)
    low = (paired - high.astype(np.float32)).astype(BF16)
    return high, low


def forward_table():
    high, low = paired_table()
    return np.block([[high.T, low.T], [high.T, np.zeros_like(low)]]).astype(BF16)


def inverse_table():
    high, low = paired_table()
    return np.block([[high, low], [high, np.zeros_like(low)]]).astype(BF16)


def split(x):
    high = x.astype(BF16)
    low = (x - high.astype(F32)).astype(BF16)
    return jnp.concatenate([high, low], axis=1)


def product(x, table):
    out = jnp.dot(x, table, preferred_element_type=F32)
    return out[:, :LANES] + out[:, LANES:]


def unpack(raw, wanted):
    count = len(wanted)
    size = raw.shape[-1] // PIECES
    rows = size // LANES
    step = min(rows, 128)

    def kernel(raw_ref, *outs):
        me = lax.axis_index("fsdp")
        chip, core = me // CORES, lax.rem(me, CORES)
        for i, (n, other) in enumerate(wanted):
            lane = lax.rem(core + other, CORES)
            to = (chip, chip + 1 - 2 * lax.rem(chip, 2), lax.rem(chip + 2, 4), 3 - chip)[n]
            start = (to * CORES + lane) * size
            for k in range(rows // step):
                at = pl.multiple_of(start + k * step * LANES, step * LANES)
                some = raw_ref[0, :, pl.ds(at, step * LANES)]
                outs[i][pl.ds(k * step, step), :] = some.reshape(step, LANES)

    return pl.pallas_call(
        kernel,
        in_specs=[VMEM],
        out_specs=[VMEM] * count,
        out_shape=[jax.ShapeDtypeStruct((rows, LANES), BF16)] * count,
        compiler_params=pltpu.CompilerParams(vmem_limit_bytes=VMEM_LIMIT),
        cost_estimate=pl.CostEstimate(flops=0, bytes_accessed=count * size * 6, transcendentals=0),
    )(raw)


def local_kernel(kernel, shapes, *args, scratch=()):
    return pl.pallas_call(
        kernel,
        in_specs=[VMEM] * len(args),
        out_specs=[VMEM] * len(shapes),
        out_shape=[jax.ShapeDtypeStruct(s, t) for s, t in shapes],
        scratch_shapes=[pltpu.VMEM(s, t) for s, t in scratch],
        compiler_params=pltpu.CompilerParams(vmem_limit_bytes=VMEM_LIMIT),
        cost_estimate=pl.CostEstimate(
            flops=0, bytes_accessed=sum(a.size * a.dtype.itemsize for a in args), transcendentals=0
        ),
    )(*args)


def far_kernel(mine_ref, given_ref, low_ref, high_ref):
    half = low_ref.shape[0]
    for at, out in ((0, low_ref), (half, high_ref)):
        some = pl.ds(at, half)
        out[...] = (mine_ref[some, :].astype(F32) + given_ref[some, :].astype(F32)).astype(BF16)


def near_kernel(mine1_ref, given1_ref, mine3_ref, given3_ref, near1_ref, near3_ref, sum1_ref, sum3_ref):
    half = near1_ref.shape[0]
    low, high = pl.ds(0, half), pl.ds(half, half)
    near1_ref[...] = (mine1_ref[low, :].astype(F32) + given1_ref[low, :].astype(F32)).astype(BF16)
    near3_ref[...] = (mine3_ref[high, :].astype(F32) + given3_ref[high, :].astype(F32)).astype(BF16)
    sum1_ref[...] = mine1_ref[high, :].astype(F32) + given1_ref[high, :].astype(F32)
    sum3_ref[...] = mine3_ref[low, :].astype(F32) + given3_ref[low, :].astype(F32)


def last_kernel(sum_ref, far_ref, out_ref):
    out_ref[...] = (sum_ref[...] + far_ref[...].astype(F32)).astype(BF16)


def list_kernel(bands_ref, counts_ref, _, hot_ref, ranks_ref, pick_ref):
    blocks = bands_ref.shape[1]
    for k in range(blocks // LANES):
        some = pl.ds(k * LANES, LANES)
        slots = lax.broadcasted_iota(jnp.int32, (KMAX, LANES), 0)
        place = jnp.where(slots < counts_ref[:, some], bands_ref[:, some], -LANES)
        freqs = lax.broadcasted_iota(jnp.int32, (SEG, LANES), 0)
        rank = jnp.zeros((SEG, LANES), jnp.int32)
        for j in range(KMAX):
            rank = jnp.where(freqs == place[j : j + 1], j + 1, rank)
        rank = rank.astype(F32)
        rank = jnp.concatenate([rank, rank], axis=0).T
        place = place.astype(F32)
        place = jnp.concatenate([place, place + SEG, place, place + SEG], axis=0).T
        hot_ref[some, :] = rank
        first = lax.broadcasted_iota(jnp.int32, (SUB, LANES), 1) < SEG
        for p in range(LANES // (2 * SUB)):
            at = p * 2 * SUB
            out = pl.ds(k * (LANES // 2) + p * SUB, SUB)
            ranks_ref[out, :] = jnp.where(first, rank[at : at + SUB], rank[at + SUB : at + 2 * SUB])
            both = jnp.where(first, place[at : at + SUB], place[at + SUB : at + 2 * SUB])
            pick_ref[out, :] = both.astype(jnp.int32)


def base_kernel(mom_ref, mine_ref, given_ref, low_ref, high_ref, hot_ref, fwd_ref, inv_ref, out_ref, mask_ref):
    half = low_ref.shape[0]
    for at, part in ((0, low_ref), (half, high_ref)):
        some = pl.ds(at, half)
        out_ref[some, :] = (
            0.999 * mom_ref[some, :]
            + mine_ref[some, :].astype(F32)
            + given_ref[some, :].astype(F32)
            + part[...].astype(F32)
        )
    blocks = hot_ref.shape[0]
    hot = hot_ref[...].astype(F32)
    for q in range(QUADS):
        mask_ref[pl.ds(q, blocks, stride=QUADS), :] = hot


def guess_kernel(base_ref, fwd_ref, coeff_ref):
    rows = base_ref.shape[0]
    step = min(rows, 256)
    for k in range(rows // step):
        some = pl.ds(k * step, step)
        coeff_ref[some, :] = product(split(base_ref[some, :]), fwd_ref[...])


def lane_gather(x, index):
    return jnp.take_along_axis(x, index, axis=1, mode="promise_in_bounds")


def keep_kernel(coeff_ref, low_ref, high_ref, mask_ref, pick_ref, rank_ref, fwd_ref, sent_ref, pack_ref, held_ref):
    half = low_ref.shape[0]
    piece = 2 * SUB * QUADS
    step = min(half, 256)
    first = lax.broadcasted_iota(jnp.int32, (SUB, LANES), 1) < SEG
    for at, part in ((0, low_ref), (half, high_ref)):
        for k in range(half // step):
            start = at + k * step
            some = pl.ds(start, step)
            coeff = coeff_ref[some, :] + product(part[pl.ds(k * step, step), :], fwd_ref[:LANES, :])
            held_ref[some, :] = coeff
            sent_ref[some, :] = jnp.where(mask_ref[some, :] > 0.5, coeff, 0.0).astype(BF16)
            for p in range(start // piece, (start + step) // piece):
                pick = pick_ref[pl.ds(p * SUB, SUB), :]
                index = jnp.maximum(pick, 0)
                out = []
                for q in range(QUADS):
                    one = held_ref[pl.ds(p * piece + q, SUB, stride=QUADS), :]
                    two = held_ref[pl.ds(p * piece + piece // 2 + q, SUB, stride=QUADS), :]
                    both = jnp.where(first, lane_gather(one, index), lane_gather(two, index))
                    out.append(jnp.where(pick >= 0, both, 0.0))
                out.append(rank_ref[pl.ds(p * SUB, SUB), :])
                pack_ref[p] = jnp.concatenate(out, axis=0).astype(BF16)


def remove_kernel(sent_ref, base_ref, low_ref, high_ref, inv_ref, new_ref):
    half = low_ref.shape[0]
    step = min(half, 256)
    for at, part in ((0, low_ref), (half, high_ref)):
        for k in range(half // step):
            some = pl.ds(at + k * step, step)
            moment = base_ref[some, :] + part[pl.ds(k * step, step), :].astype(F32)
            new_ref[some, :] = moment - product(sent_ref[some, :], inv_ref[:LANES, :])


def combine_kernel(factor, pieces_ref, inv_ref, out_ref, held_ref):
    first = lax.broadcasted_iota(jnp.int32, (SUB, LANES), 1) < SEG
    shift = jnp.where(first, -1, KMAX - 1)
    totals = [jnp.zeros((SUB, LANES), F32) for _ in range(2 * QUADS)]
    for r in range(pieces_ref.shape[0]):
        piece = pieces_ref[r].astype(F32)
        rank = piece[SUB * QUADS :]
        other = pltpu.roll(rank, SEG, axis=1)
        for h in range(2):
            place = jnp.where(first, rank, other) if h == 0 else jnp.where(first, other, rank)
            index = jnp.maximum(place.astype(jnp.int32) + shift, 0) + h * SEG
            for q in range(QUADS):
                value = lane_gather(piece[q * SUB : (q + 1) * SUB], index)
                totals[h * QUADS + q] += jnp.where(place > 0.5, value, 0.0)
    back = product(split(jnp.concatenate(totals, axis=0)), inv_ref[...]) * factor
    for h in range(2):
        for q in range(QUADS):
            at = (h * QUADS + q) * SUB
            held_ref[pl.ds(h * SUB * QUADS + q, SUB, stride=QUADS), :] = back[at : at + SUB]
    out_ref[...] = jnp.broadcast_to(held_ref[...].astype(BF16)[None], out_ref.shape)


def spread_kernel(zs, *refs):
    planes, out_ref = refs[:-1], refs[-1]
    count = planes[0].shape[0]
    x = lax.axis_index("rep") // zs
    order = (x, x + 1 - 2 * lax.rem(x, 2), lax.rem(x + 2, 4), 3 - x)
    for n, ref in enumerate(planes):
        out_ref[pl.ds(pl.multiple_of(order[n] * count, count), count), :] = ref[...].astype(F32)


def body(grad_parts, momentum, bands, counts):
    replicas = lax.axis_size("rep")
    holders = lax.axis_size("fsdp")
    forward, inverse = jnp.asarray(forward_table()), jnp.asarray(inverse_table())

    blocks = momentum.size // (GROUP * SEG)
    rows = momentum.size // LANES
    half = rows // 2

    whole, part = (rows, LANES), (half, LANES)

    def over_cores(x):
        return lax.ppermute(x, "fsdp", [(f, f ^ 1) for f in range(holders)])

    def trade(x, n):
        return lax.ppermute(x, "fsdp", [(f, f ^ (CORES * n)) for f in range(holders)])

    (theirs2,) = unpack(grad_parts, ((2, 1),))
    given2 = over_cores(theirs2)
    mine2, theirs1, theirs3, mine1, mine3, theirs0, mine0 = unpack(
        grad_parts, ((2, 0), (1, 1), (3, 1), (1, 0), (3, 0), (0, 1), (0, 0))
    )
    given1, given3 = over_cores(theirs1), over_cores(theirs3)
    far1, far3 = local_kernel(far_kernel, [(part, BF16)] * 2, mine2, given2)
    far1, far3 = trade(far1, 1), trade(far3, 3)
    given0 = over_cores(theirs0)
    near1, near3, sum1, sum3 = local_kernel(
        near_kernel, [(part, BF16)] * 2 + [(part, F32)] * 2, mine1, given1, mine3, given3
    )
    near_low, near_high = trade(near1, 1), trade(near3, 3)
    (last3,) = local_kernel(last_kernel, [(part, BF16)], sum3, far1)
    last_low = trade(last3, 3)
    (last1,) = local_kernel(last_kernel, [(part, BF16)], sum1, far3)
    last_high = trade(last1, 1)

    hot, ranks, pick = pl.pallas_call(
        list_kernel,
        in_specs=[VMEM, VMEM, pl.BlockSpec(memory_space=pl.ANY)],
        out_specs=[VMEM] * 3,
        out_shape=[
            jax.ShapeDtypeStruct((blocks, LANES), F32),
            jax.ShapeDtypeStruct((blocks // 2, LANES), F32),
            jax.ShapeDtypeStruct((blocks // 2, LANES), jnp.int32),
        ],
        compiler_params=pltpu.CompilerParams(vmem_limit_bytes=VMEM_LIMIT),
    )(bands.reshape(blocks, KMAX).T, counts, near_low)

    base, mask = local_kernel(
        base_kernel,
        [(whole, F32)] * 2,
        momentum.reshape(whole),
        mine0,
        given0,
        near_low,
        near_high,
        hot,
        forward,
        inverse,
    )
    (coeff,) = local_kernel(guess_kernel, [(whole, F32)], base, forward)
    sent, pack = local_kernel(
        keep_kernel,
        [(whole, BF16), ((replicas, SUB * (QUADS + 1), LANES), BF16)],
        coeff,
        last_low,
        last_high,
        mask,
        pick,
        ranks,
        forward,
        scratch=[(whole, F32)],
    )
    (new,) = local_kernel(remove_kernel, [(whole, F32)], sent, base, last_low, last_high, inverse)

    pieces = lax.all_to_all(pack, "rep", split_axis=0, concat_axis=0, tiled=True)
    xs = 4
    zs = replicas // xs
    (mixed,) = local_kernel(
        lambda *refs: combine_kernel(1.0 / math.sqrt(replicas), *refs),
        [((zs, 2 * SUB * QUADS, LANES), BF16)],
        pieces,
        inverse,
        scratch=[((2 * SUB * QUADS, LANES), F32)],
    )
    lines = [[zs * x + z for z in range(zs)] for x in range(xs)]
    plane = lax.all_to_all(
        mixed, "rep", split_axis=0, concat_axis=0, axis_index_groups=lines, tiled=True
    ).reshape(rows // xs, LANES)

    def across(n):
        return lax.ppermute(plane, "rep", [(r, r ^ (zs * n)) for r in range(replicas)])

    planes = [plane] + [across(n) for n in (1, 2, 3)]
    (update,) = local_kernel(lambda *refs: spread_kernel(zs, *refs), [(whole, F32)], *planes)
    return (new.reshape(momentum.shape), update.reshape(-1))


def solution(mesh):
    placed = (P("rep", "fsdp", None), P("rep", "fsdp"), P("rep", "fsdp", None), P("rep", "fsdp"))
    return jax.shard_map(
        body, mesh=mesh, in_specs=placed, out_specs=(P("rep", "fsdp"), P("fsdp")), check_vma=False
    )
```
